128 devices in a mesh: row: 8 (over y, z_lo), col: 16 (over z_hi, x, core).
Axes of the slice: x: 4, y: 4, z: 4 (z_hi: 2, z_lo: 2; z = z_hi * 2 + z_lo), core: 2. Of those that a mesh axis runs over, the one named last changes fastest.
Arguments:
- a_values: bfloat16 [64, 16, 128, 128], P('row', 'col'), may hold values from -6 to 6
- a_blocks: int32 [64, 16], P('row', 'col'), may hold values from 0 to 511, as said below
- a_live: int32 [64, 16], P('row', 'col'), may hold values from 0 to 1, as said below
- b_values: bfloat16 [512, 16, 128, 128], P('row', 'col'), may hold values from -0.5 to 0.5
- b_columns: int32 [512, 16], P('row', 'col'), may hold values from 0 to 1023, as said below
- filter_mask: int32 [64, 1024], P('row', 'col'), may hold values 0 or 1
Outputs:
- product: bfloat16 [64, 1024, 128, 128], P('row', 'col')
The draws below stay inside these ranges and needn't reach their ends.
Inputs may be any that keep to these rules, and one draw needn't show every extreme that they name: `a_blocks`: the 16 entries of a block row are distinct. `a_live`: every block row has at least one live slot; some block row has all 16 live. `b_columns`: in a contraction row, slot g names a block column between g * 64 and (g + 1) * 64 - 1, so the slot held by index g of col always falls in that index's block columns.
All inputs are finite; a program needn't handle non-finite values. No bound on the sum of `filter_mask` on one device may be relied on, other than what follows from the above.
Results may differ from the reference program's by a relative error of at most 0.001.
Values may be sent and summed in bfloat16 or wider, within the bound.
No kernel may reach another device: no remote copies, remote signals or barrier semaphores. Data moves between devices by JAX's collectives and lax.ppermute only.
A program may use at most 192 MiB of HBM per device.

```python
import jax
import jax.numpy as jnp
from jax import lax

BS = 128
BC_DEV = 64
SB_DEV = 1
NBR = 64
NBC = 1024
KW = 512
SLOTS_A = 16
SLOTS_B = 16


def distinct_pick(key, row_count, choice_count, taken):
    scores = jax.random.randint(key, (row_count, choice_count), 0, 2 ** 20) * choice_count + jnp.arange(choice_count)
    ordering = jnp.argsort(scores, axis=1, stable=True)
    return ordering[:, :taken].astype(jnp.int32)


def draw_a_blocks(key, part):
    key = jax.random.fold_in(key, 11)
    return distinct_pick(key, NBR, KW, SLOTS_A)


def draw_a_live(key, part):
    key = jax.random.fold_in(key, 12)
    key_count, key_full, key_rank = jax.random.split(key, 3)
    counts = 1 + jax.random.randint(key_count, (NBR,), 0, SLOTS_A)
    full_row = jax.random.randint(key_full, (), 0, NBR)
    counts = jnp.where(jnp.arange(NBR) == full_row, SLOTS_A, counts)
    ordering = distinct_pick(key_rank, NBR, SLOTS_A, SLOTS_A)
    ranking = jnp.argsort(ordering, axis=1)
    return (ranking < counts[:, None]).astype(jnp.int32)


def draw_b_columns(key, part):
    key = jax.random.fold_in(key, 13)
    groups = NBC // BC_DEV
    picked = distinct_pick(key, KW * groups, BC_DEV, SB_DEV).reshape(KW, groups, SB_DEV)
    offsets = (jnp.arange(groups) * BC_DEV)[None, :, None]
    return (picked + offsets).reshape(KW, groups * SB_DEV).astype(jnp.int32)


def with_ends(result, rng, least, largest):
    dims = result.shape
    place = [jax.random.randint(jax.random.fold_in(rng, axis), (), 0, dims[axis]) for axis in range(len(dims))]
    result = result.at[tuple(place)].set(least)
    longest = dims.index(max(dims))
    place[longest] = (place[longest] + 1) % dims[longest]
    return result.at[tuple(place)].set(largest)


def block_scale(rng, extent, cuts, smallest, high):
    level = 1.0
    for axis_at, shards_of in cuts:
        draws = jax.random.uniform(jax.random.fold_in(jax.random.fold_in(rng, 6), axis_at), (shards_of,), jnp.float32, smallest / len(cuts), high / len(cuts))
        level = level * jnp.repeat(jnp.exp(draws), extent[axis_at] // shards_of).reshape((-1,) + (1,) * (len(extent) - 1 - axis_at))
    return level


def scatter_about(rng, shape, deviation, reach, pieces=(), held_as=jnp.bfloat16):
    factor_of = block_scale(rng, shape, pieces, -0.22, 0.18) if pieces else 1.0
    array = jax.random.normal(rng, shape, jnp.float32) * deviation * factor_of
    return jnp.minimum(jnp.maximum(array, -reach), reach).astype(held_as)


def setup_inputs(seed: int = 0) -> dict:
    key_of = jax.random.split(jax.random.key(seed), 7)
    a_values = scatter_about(key_of[0], (NBR, SLOTS_A, BS, BS), 1.0, 6.0, ((0, 8), (1, 16)))
    a_blocks = draw_a_blocks(jax.random.fold_in(key_of[6], 71), 0)
    a_live = draw_a_live(jax.random.fold_in(key_of[6], 71), 0)
    b_values = scatter_about(key_of[3], (KW, SLOTS_B, BS, BS), BS ** -0.5, 0.5, ((0, 8), (1, 16)))
    b_columns = draw_b_columns(jax.random.fold_in(key_of[6], 71), 0)
    filter_mask = with_ends((jax.random.randint(key_of[5], (NBR, NBC), 0, 4) < 3).astype(jnp.int32), jax.random.fold_in(key_of[5], 1), 0, 1)
    return dict(a_values=a_values, a_blocks=a_blocks, a_live=a_live, b_values=b_values, b_columns=b_columns, filter_mask=filter_mask)


def reference(a_values, a_blocks, a_live, b_values, b_columns, filter_mask):
    def one_row(element):
        values_row, blocks_row, alive_row, mask_row = element
        chosen = jnp.take(b_values, blocks_row, axis=0).astype(jnp.float32)
        targets = jnp.take(b_columns, blocks_row, axis=0)
        products = jnp.einsum("amn,abnp->abmp", values_row.astype(jnp.float32), chosen, precision=lax.Precision.HIGHEST)
        products = products * alive_row.astype(jnp.float32)[:, None, None, None]
        summed = jax.ops.segment_sum(products.reshape((-1,) + products.shape[2:]), targets.reshape(-1), num_segments=NBC)
        return (summed * mask_row.astype(jnp.float32)[:, None, None]).astype(jnp.bfloat16)
    return lax.map(one_row, (a_values, a_blocks, a_live, filter_mask))
```

```python
import functools

import jax
import jax.numpy as jnp
from jax import lax
from jax.experimental import pallas as pl
from jax.experimental.pallas import tpu as pltpu
from jax.sharding import Mesh, PartitionSpec as P

BS = 128
ROWS = 8
COLS = 16
RB = 8
KB = 64
JB = 64
SLOTS = 16
LANES = 128
CAPS = (12, 14, 16, 18, 20)
R_AXES = ("y", "zl")
C_AXES = ("zh", "x", "core")

SEND = 0
META = 8
KEYS = 16
RANK = 32
MISC = 36
INFO = 40

LEFT, SOURCE, PLACE, COL, HEAD, COUNT = 0, 16, 32, 48, 64, 96
UNROLL = 4


def list_kernel(me_ref, meta_ref, info_ref, which_ref):
    me_r, me_c = me_ref[0], me_ref[1]
    lane = lax.broadcasted_iota(jnp.int32, (LANES, LANES), 1)
    sub8 = lax.broadcasted_iota(jnp.int32, (ROWS, LANES), 0)
    lane8 = lax.broadcasted_iota(jnp.int32, (ROWS, LANES), 1)
    tri_a = lax.broadcasted_iota(jnp.int32, (LANES, LANES), 0)
    before = ((tri_a < lane) & (tri_a // KB == lane // KB)).astype(jnp.float32)
    keys = meta_ref[:, 0:RB]
    top = jnp.zeros((ROWS, LANES), jnp.int32)

    def needed(base):
        hit = jnp.zeros((LANES, LANES), jnp.int32)
        for i in range(RB):
            hit = jnp.where(keys[:, i:i + 1] == lane + base, 1, hit)
        need = jnp.max(hit.reshape(ROWS, COLS, LANES), axis=1)
        rank = jnp.dot(need.astype(jnp.float32), before, preferred_element_type=jnp.float32)
        return need, rank.astype(jnp.int32)

    info_ref[...] = jnp.zeros((INFO, LANES), jnp.int32)
    for q in range(ROWS * KB // LANES):
        need, rank = needed(q * LANES)
        owner = (lane8 + q * LANES) // KB
        top = jnp.maximum(top, jnp.where(owner == sub8, 0, need + rank))
        mine = jnp.sum(jnp.where(sub8 == me_r, rank, 0), axis=0, keepdims=True)
        info_ref[RANK + q:RANK + q + 1, :] = mine
    largest = jnp.max(top)
    which_ref[0] = sum((largest > cap).astype(jnp.int32) for cap in CAPS)
    info_ref[MISC:MISC + 1, :] = jnp.where(
        lane8[0:1] == 0, largest, jnp.where(lane8[0:1] == 1, me_r, me_c))

    need, rank = needed(me_r * KB)
    need = jnp.where((lane8 < KB) & (sub8 != me_r), need, 0)
    counts = jnp.sum(need, axis=1, keepdims=True)

    def place(s, lists):
        here = jnp.sum(jnp.where((need == 1) & (rank == s), lane8, 0), axis=1, keepdims=True)
        return jnp.where(lane8 == s, here, lists)

    lists = lax.fori_loop(0, largest, place, jnp.zeros((ROWS, LANES), jnp.int32))
    info_ref[SEND:SEND + ROWS, :] = jnp.where(lane8 == LANES - 1, counts, lists)
    for src in range(ROWS):
        info_ref[META + src:META + src + 1, :] = meta_ref[pl.ds(src * COLS + me_c, 1), :]
    info_ref[KEYS:KEYS + SLOTS, :] = meta_ref[pl.ds(pl.multiple_of(me_r * COLS, COLS), COLS), :]


def make_lists(me, meta):
    return pl.pallas_call(
        list_kernel,
        out_shape=(
            jax.ShapeDtypeStruct((INFO, LANES), jnp.int32),
            jax.ShapeDtypeStruct((1,), jnp.int32),
        ),
        in_specs=[
            pl.BlockSpec(memory_space=pltpu.SMEM),
            pl.BlockSpec(memory_space=pltpu.VMEM),
        ],
        out_specs=(
            pl.BlockSpec(memory_space=pltpu.VMEM),
            pl.BlockSpec(memory_space=pltpu.SMEM),
        ),
        name="make_lists",
    )(me, meta)


def pack_kernel(cap, first, info_ref, b_ref, out_ref, sems):
    def each(dest, go):
        count = jnp.minimum(info_ref[SEND + dest, LANES - 1] - first, cap)

        @pl.loop(0, count)
        def _(s):
            block = info_ref[SEND + dest, first + s]
            go(pltpu.make_async_copy(b_ref.at[block], out_ref.at[dest, s], sems.at[dest, s]))

    @pl.loop(0, ROWS)
    def _(dest):
        each(dest, lambda copy: copy.start())

    @pl.loop(0, ROWS)
    def _(dest):
        each(dest, lambda copy: copy.wait())


def pack(cap, first, info, b):
    return pl.pallas_call(
        functools.partial(pack_kernel, cap, first),
        out_shape=jax.ShapeDtypeStruct((ROWS, cap, BS, BS), jnp.bfloat16),
        in_specs=[
            pl.BlockSpec(memory_space=pltpu.SMEM),
            pl.BlockSpec(memory_space=pltpu.VMEM),
        ],
        out_specs=pl.BlockSpec(memory_space=pl.ANY),
        scratch_shapes=[pltpu.SemaphoreType.DMA((ROWS, cap))],
        compiler_params=pltpu.CompilerParams(vmem_limit_bytes=8 << 20),
        name="pack_blocks",
    )(info, b)


def plan_kernel(info_ref, mask_ref, plan_ref, head_of):
    me_r, me_c = info_ref[MISC, 1], info_ref[MISC, 2]

    @pl.loop(0, RB)
    def _(i):
        @pl.loop(0, JB)
        def _(j):
            head_of[j] = -1

        plan_ref[i, COUNT] = 0

        @pl.loop(0, SLOTS)
        def _(a):
            key = info_ref[KEYS + a, i]

            @pl.when(key >= 0)
            def _():
                src, block = key // KB, lax.rem(key, KB)
                col = info_ref[META + src, RB + block]

                @pl.when(mask_ref[i, col] != 0)
                def _():
                    n = plan_ref[i, COUNT]
                    head = head_of[col]
                    rank = info_ref[RANK + key // LANES, lax.rem(key, LANES)]
                    part = (a ^ me_c) & 1
                    shift = ((me_c >> 1) - (a >> 1)) & 3
                    turn = ((a ^ me_c) >> 3) & 1
                    plan_ref[i, LEFT + n] = (part * 4 + shift) * 2 + turn
                    plan_ref[i, SOURCE + n] = jnp.where(src == me_r, -1, src)
                    plan_ref[i, PLACE + n] = jnp.where(src == me_r, block, rank)
                    plan_ref[i, COL + n] = col
                    plan_ref[i, HEAD + n] = jnp.where(head < 0, n, head)
                    plan_ref[i, COUNT] = n + 1

                    @pl.when(head < 0)
                    def _():
                        head_of[col] = n


def make_plan(info, mask):
    return pl.pallas_call(
        plan_kernel,
        out_shape=jax.ShapeDtypeStruct((RB, LANES), jnp.int32),
        in_specs=[
            pl.BlockSpec(memory_space=pltpu.SMEM),
            pl.BlockSpec(memory_space=pltpu.SMEM),
        ],
        out_specs=pl.BlockSpec(memory_space=pltpu.SMEM),
        scratch_shapes=[pltpu.SMEM((JB,), jnp.int32)],
        cost_estimate=pl.CostEstimate(flops=0, bytes_accessed=8 << 20, transcendentals=0),
        name="make_plan",
    )(info, mask)


def zero_kernel(info_ref, out_ref, zeros, sems):
    zeros[...] = jnp.zeros(zeros.shape, zeros.dtype)
    copies = [
        pltpu.make_async_copy(zeros, out_ref.at[i], sems.at[i]) for i in range(RB)
    ]
    for copy in copies:
        copy.start()
    for copy in copies:
        copy.wait()


def zero_blocks(info):
    return pl.pallas_call(
        zero_kernel,
        out_shape=jax.ShapeDtypeStruct((RB, JB, BS, BS), jnp.bfloat16),
        in_specs=[pl.BlockSpec(memory_space=pl.ANY)],
        out_specs=pl.BlockSpec(memory_space=pl.ANY),
        scratch_shapes=[
            pltpu.VMEM((JB, BS, BS), jnp.bfloat16),
            pltpu.SemaphoreType.DMA((RB,)),
        ],
        compiler_params=pltpu.CompilerParams(vmem_limit_bytes=8 << 20),
        cost_estimate=pl.CostEstimate(flops=0, bytes_accessed=16 << 20, transcendentals=0),
        name="zero_blocks",
    )(info)


def product_kernel(plan_ref, *refs):
    left_refs, (got_ref, b_ref, _, out_ref) = refs[:8], refs[8:12]
    a_buf, b_buf, res, acc, a_sems, b_sems, out_sems = refs[12:]

    for n, ref in enumerate(left_refs):
        pltpu.make_async_copy(ref, a_buf.at[pl.ds(2 * n, 2)], a_sems.at[n]).start()

    @pl.loop(0, RB)
    def _(i):
        @pl.loop(0, plan_ref[i, COUNT])
        def _(n):
            src, place = plan_ref[i, SOURCE + n], plan_ref[i, PLACE + n]

            @pl.when(src < 0)
            def _():
                pltpu.make_async_copy(b_ref.at[place], b_buf.at[i, n], b_sems.at[i, n]).start()

            @pl.when(src >= 0)
            def _():
                pltpu.make_async_copy(got_ref.at[src, place], b_buf.at[i, n], b_sems.at[i, n]).start()

    for n, ref in enumerate(left_refs):
        pltpu.make_async_copy(ref, a_buf.at[pl.ds(2 * n, 2)], a_sems.at[n]).wait()

    def write(i, n):
        return pltpu.make_async_copy(res.at[i, n], out_ref.at[i, plan_ref[i, COL + n]], out_sems.at[i, n])

    @pl.loop(0, RB)
    def _(i):
        count = plan_ref[i, COUNT]

        @pl.loop(0, (count + UNROLL - 1) // UNROLL)
        def _(step):
            sums = []
            for u in range(UNROLL):
                n = step * UNROLL + u
                within = n < count

                @pl.when(within)
                def _():
                    pltpu.make_async_copy(b_ref.at[0], b_buf.at[i, n], b_sems.at[i, n]).wait()

                left = jnp.where(within, plan_ref[i, LEFT + n], 0)
                head = jnp.where(within, plan_ref[i, HEAD + n], SLOTS)
                sums.append((n, head, jnp.dot(
                    a_buf[left, i], b_buf[i, n], preferred_element_type=jnp.float32)))
            for n, head, total in sums:
                total = total + jnp.where(head != n, acc[head], 0.0)
                acc[head] = total
                res[i, head] = total.astype(jnp.bfloat16)

        @pl.loop(0, count)
        def _(n):
            @pl.when(plan_ref[i, HEAD + n] == n)
            def _():
                write(i, n).start()

    @pl.loop(0, RB)
    def _(i):
        @pl.loop(0, plan_ref[i, COUNT])
        def _(n):
            @pl.when(plan_ref[i, HEAD + n] == n)
            def _():
                write(i, n).wait()


def products(plan, left, got, b, blank):
    return pl.pallas_call(
        product_kernel,
        out_shape=jax.ShapeDtypeStruct((RB, JB, BS, BS), jnp.bfloat16),
        in_specs=[pl.BlockSpec(memory_space=pltpu.SMEM)] + [pl.BlockSpec(memory_space=pl.ANY)] * 11,
        out_specs=pl.BlockSpec(memory_space=pl.ANY),
        input_output_aliases={11: 0},
        scratch_shapes=[
            pltpu.VMEM((SLOTS, RB, BS, BS), jnp.bfloat16),
            pltpu.VMEM((RB, SLOTS, BS, BS), jnp.bfloat16),
            pltpu.VMEM((RB, SLOTS + 1, BS, BS), jnp.bfloat16),
            pltpu.VMEM((SLOTS + 1, BS, BS), jnp.float32),
            pltpu.SemaphoreType.DMA((8,)),
            pltpu.SemaphoreType.DMA((RB, SLOTS)),
            pltpu.SemaphoreType.DMA((RB, SLOTS)),
        ],
        compiler_params=pltpu.CompilerParams(vmem_limit_bytes=24 << 20),
        name="block_products",
    )(plan, *left, got, b, blank)


def per_device(a_values, a_blocks, a_live, b_values, b_columns, filter_mask):
    me_r, me_c = lax.axis_index(R_AXES), lax.axis_index(C_AXES)
    keys = jnp.where(a_live != 0, a_blocks, -1)[:, 0]
    record = jnp.concatenate([keys, b_columns[:, 0] - me_c * JB])
    record = jnp.pad(record, (0, LANES - record.shape[0]))
    meta = lax.all_to_all(
        jnp.broadcast_to(record[None, :], (ROWS * COLS, LANES)), R_AXES + C_AXES, 0, 0, tiled=True)
    a = a_values.reshape(RB, BS, BS)
    b = b_values.reshape(KB, BS, BS)
    across = lax.ppermute(a, "zh", [(0, 1), (1, 0)])
    info, which = make_lists(jnp.stack([me_r, me_c]).astype(jnp.int32), meta)

    def exchange(cap, first, info, b):
        return lax.all_to_all(pack(cap, first, info, b), R_AXES, 0, 0)

    def finish(info, mask, a, across, b, got):
        pair = jnp.stack([a, across])
        along = [pair] + [
            lax.ppermute(pair, "x", [(i, (i + s) % 4) for i in range(4)]) for s in range(1, 4)]
        left = along + [lax.ppermute(part, "core", [(0, 1), (1, 0)]) for part in along]
        return products(make_plan(info, mask), left, got, b, zero_blocks(info))

    def one_round(cap, info, mask, a, across, b):
        packed = pack(cap, 0, info, b)
        packed, a, across, info = lax.optimization_barrier((packed, a, across, info))
        got = lax.all_to_all(packed, R_AXES, 0, 0)
        return finish(info, mask, a, across, b, got)

    def rounds(info, mask, a, across, b):
        cap = CAPS[-1]
        got = [exchange(cap, first, info, b) for first in range(0, KB, cap)]
        return finish(info, mask, a, across, b, jnp.concatenate(got, axis=1))

    branches = [functools.partial(one_round, cap) for cap in CAPS] + [rounds]
    return lax.switch(which[0], branches, info, filter_mask, a, across, b)


def solution(mesh):
    fine = Mesh(mesh.devices.reshape(4, 2, 2, 4, 2), R_AXES + C_AXES)
    pair = P(R_AXES, C_AXES)
    blocks = P(R_AXES, C_AXES, None, None)
    return jax.shard_map(
        per_device, mesh=fine, in_specs=(blocks, pair, pair, blocks, pair, pair),
        out_specs=blocks, check_vma=False
    )
```

```python
import functools

import jax
import jax.numpy as jnp
from jax import lax
from jax.experimental import pallas as pl
from jax.experimental.pallas import tpu as pltpu
from jax.sharding import Mesh, PartitionSpec as P

BS = 128
ROWS = 8
COLS = 16
RB = 8
KB = 64
JB = 64
SLOTS = 16
LANES = 128
CAPS = (12, 13, 14, 15, 16, 17, 18, 19, 20)
R_AXES = ("y", "zl")
C_AXES = ("zh", "x", "core")
UNROLL = 4

LOCAL = 8
PLAN_COUNT = 1


def record_kernel(base_ref, blocks_ref, live_ref, cols_ref, out_ref):
    keys = jnp.where(live_ref[...] != 0, blocks_ref[...], -1)
    row = jnp.concatenate(
        [keys, jnp.zeros((1, LANES - KB - RB), jnp.int32), cols_ref[...] - base_ref[0]], axis=1)
    out_ref[...] = jnp.broadcast_to(row.reshape(1, 1, LANES), out_ref.shape)


def make_record(base, blocks, live, cols):
    vmem = pl.BlockSpec(memory_space=pltpu.VMEM)
    return pl.pallas_call(
        record_kernel,
        out_shape=jax.ShapeDtypeStruct((ROWS * COLS, 1, LANES), jnp.int32),
        in_specs=[pl.BlockSpec(memory_space=pltpu.SMEM), vmem, vmem, vmem],
        out_specs=vmem,
        name="make_record",
    )(base, blocks, live, cols)


def list_kernel(r_ref, c_ref, meta_ref, mask_ref, a_ref, z_ref, k_ref, zk_ref,
                send_ref, plan_ref, which_ref, quad_ref, table_ref, quad_sems):
    copies = [
        pltpu.make_async_copy(ref, quad_ref.at[n], quad_sems.at[n])
        for n, ref in enumerate((a_ref, z_ref, k_ref, zk_ref))
    ]
    for copy in copies:
        copy.start()
    me_r, me_c = r_ref[0], c_ref[0]
    lane = lax.broadcasted_iota(jnp.int32, (LANES, LANES), 1)
    sub8 = lax.broadcasted_iota(jnp.int32, (ROWS, LANES), 0)
    lane8 = lax.broadcasted_iota(jnp.int32, (ROWS, LANES), 1)
    above = lax.broadcasted_iota(jnp.int32, (LANES, LANES), 0)
    before = ((above < lane) & (above // KB == lane // KB)).astype(jnp.float32)
    keys = meta_ref[:, 0:RB]
    top = jnp.zeros((ROWS, LANES), jnp.int32)

    def needed(base):
        hit = jnp.zeros((LANES, LANES), jnp.int32)
        for i in range(RB):
            hit = jnp.where(keys[:, i:i + 1] == lane + base, 1, hit)
        need = jnp.max(hit.reshape(ROWS, COLS, LANES), axis=1)
        rank = jnp.dot(need.astype(jnp.float32), before, preferred_element_type=jnp.float32)
        return need, rank.astype(jnp.int32)

    for q in range(ROWS * KB // LANES):
        need, rank = needed(q * LANES)
        owner = (lane8 + q * LANES) // KB
        top = jnp.maximum(top, jnp.where(owner == sub8, 0, need + rank))
        mine = jnp.sum(jnp.where(sub8 == me_r, rank, 0), axis=0, keepdims=True)
        low = meta_ref[pl.ds(2 * q * COLS + me_c, 1), :]
        high = meta_ref[pl.ds((2 * q + 1) * COLS + me_c, 1), :]
        cols = jnp.where(lane8[0:1] < KB, pltpu.roll(low, KB, 1), high)
        table_ref[q:q + 1, :] = mine * JB + cols
    largest = jnp.max(top)
    which_ref[0] = sum((largest > cap).astype(jnp.int32) for cap in CAPS)

    need, rank = needed(me_r * KB)
    need = jnp.where((lane8 < KB) & (sub8 != me_r), need, 0)
    counts = jnp.sum(need, axis=1, keepdims=True)

    def place(step, lists):
        for u in range(8):
            s = step * 8 + u
            here = jnp.sum(jnp.where((need == 1) & (rank == s), lane8, 0), axis=1, keepdims=True)
            lists = jnp.where(lane8 == s, here, lists)
        return lists

    lists = lax.fori_loop(0, (largest + 7) // 8, place, jnp.zeros((ROWS, LANES), jnp.int32))
    send_ref[...] = jnp.where(lane8 == LANES - 1, counts, lists)

    own = meta_ref[pl.ds(pl.multiple_of(me_r * COLS, COLS), COLS), :]
    lane16 = lax.broadcasted_iota(jnp.int32, (SLOTS, LANES), 1)
    sub16 = lax.broadcasted_iota(jnp.int32, (SLOTS, LANES), 0)
    lane_j = lax.broadcasted_iota(jnp.int32, (SLOTS, JB), 1)
    found = jnp.zeros((SLOTS, LANES), jnp.int32)
    kept = jnp.zeros((SLOTS, LANES), jnp.int32)
    for i in range(RB):
        key = own[:, i:i + 1]
        seen = jnp.zeros((SLOTS, LANES), jnp.int32)
        for q in range(ROWS * KB // LANES):
            seen = jnp.where(key == lane16 + q * LANES, table_ref[q:q + 1, :], seen)
        entry = jnp.sum(seen, axis=1, keepdims=True)
        keep = jnp.sum(jnp.where(lane_j == entry % JB, mask_ref[i:i + 1, :], 0), axis=1, keepdims=True)
        found = jnp.where(lane16 == i, entry, found)
        kept = jnp.where(lane16 == i, keep, kept)
    col, rank = found % JB, found // JB
    active = ((kept != 0) & (own >= 0) & (lane16 < RB)).astype(jnp.int32)
    pos = jnp.zeros((SLOTS, LANES), jnp.int32)
    for a in range(SLOTS):
        pos = pos + jnp.where(sub16 > a, active[a:a + 1, :], 0)
    first = jnp.full((SLOTS, LANES), SLOTS, jnp.int32)
    last = jnp.zeros((SLOTS, LANES), jnp.int32)
    for a in range(SLOTS):
        same = (active[a:a + 1, :] == 1) & (col[a:a + 1, :] == col)
        first = jnp.minimum(first, jnp.where(same, pos[a:a + 1, :], SLOTS))
        last = jnp.maximum(last, jnp.where(same, pos[a:a + 1, :], 0))
    in_row = jnp.sum(active, axis=0, keepdims=True)
    start = jnp.zeros((1, LANES), jnp.int32)
    for i in range(RB):
        start = start + jnp.where(lane8[0:1] > i, in_row[:, i:i + 1], 0)
    block, source = own & (KB - 1), own >> 6
    near = source == me_r
    other = sub16 ^ me_c
    left = ((((me_c >> 1) - (sub16 >> 1)) & 3) << 2) | ((other & 1) << 1) | ((other >> 3) & 1)
    packed = (left | (jnp.where(near, LOCAL, source) << 4) | (jnp.where(near, block, rank) << 8)
              | (col << 14) | (lane16 << 20) | ((start + first) << 23)
              | (jnp.where(last == pos, 1, 0) << 30))
    at = jnp.where(active == 1, start + pos, -1)
    listed = jnp.zeros((SLOTS, LANES), jnp.int32)
    for i in range(RB):
        listed = jnp.where(at[:, i:i + 1] == lane16, packed[:, i:i + 1], listed)
    plan_ref[0:1, :] = jnp.sum(listed, axis=0, keepdims=True)
    plan_ref[1:8, :] = jnp.broadcast_to(jnp.sum(in_row, axis=1, keepdims=True), (7, LANES))
    for copy in copies:
        copy.wait()


def make_lists(me_r, me_c, meta, mask, parts):
    vmem = pl.BlockSpec(memory_space=pltpu.VMEM)
    smem = pl.BlockSpec(memory_space=pltpu.SMEM)
    return pl.pallas_call(
        list_kernel,
        out_shape=(
            jax.ShapeDtypeStruct((ROWS, LANES), jnp.int32),
            jax.ShapeDtypeStruct((8, LANES), jnp.int32),
            jax.ShapeDtypeStruct((1,), jnp.int32),
            jax.ShapeDtypeStruct((4, RB, BS, BS), jnp.bfloat16),
        ),
        in_specs=[smem, smem] + [vmem] * 6,
        out_specs=(vmem, vmem, smem, pl.BlockSpec(memory_space=pl.ANY)),
        scratch_shapes=[
            pltpu.VMEM((ROWS * KB // LANES, LANES), jnp.int32),
            pltpu.SemaphoreType.DMA((4,)),
        ],
        name="make_lists",
    )(me_r, me_c, meta, mask, *parts)


def pack_kernel(cap, first, send_ref, b_ref, out_ref, sems):
    def each(dest, go):
        count = jnp.clip(send_ref[dest, LANES - 1] - first, 0, cap)

        @pl.loop(0, count)
        def _(s):
            block = send_ref[dest, first + s]
            go(pltpu.make_async_copy(b_ref.at[block], out_ref.at[dest, s], sems.at[dest, s]))

    for dest in range(ROWS):
        each(dest, lambda copy: copy.start())
    for dest in range(ROWS):
        each(dest, lambda copy: copy.wait())


def pack(cap, first, send, b):
    return pl.pallas_call(
        functools.partial(pack_kernel, cap, first),
        out_shape=jax.ShapeDtypeStruct((ROWS, cap, BS, BS), jnp.bfloat16),
        in_specs=[
            pl.BlockSpec(memory_space=pltpu.SMEM),
            pl.BlockSpec(memory_space=pltpu.VMEM),
        ],
        out_specs=pl.BlockSpec(memory_space=pl.ANY),
        scratch_shapes=[pltpu.SemaphoreType.DMA((ROWS, cap))],
        compiler_params=pltpu.CompilerParams(vmem_limit_bytes=60 << 20),
        name="pack_blocks",
    )(send, b)


def zero_kernel(out_ref, zeros, sems):
    zeros[...] = jnp.zeros(zeros.shape, zeros.dtype)
    copies = [
        pltpu.make_async_copy(zeros, out_ref.at[i], sems.at[i]) for i in range(RB)
    ]
    for copy in copies:
        copy.start()
    for copy in copies:
        copy.wait()


def zero_blocks():
    return pl.pallas_call(
        zero_kernel,
        out_shape=jax.ShapeDtypeStruct((RB, JB, BS, BS), jnp.bfloat16),
        out_specs=pl.BlockSpec(memory_space=pl.ANY),
        scratch_shapes=[
            pltpu.VMEM((JB, BS, BS), jnp.bfloat16),
            pltpu.SemaphoreType.DMA((RB,)),
        ],
        compiler_params=pltpu.CompilerParams(vmem_limit_bytes=8 << 20),
        cost_estimate=pl.CostEstimate(flops=0, bytes_accessed=16 << 20, transcendentals=0),
        name="zero_blocks",
    )()


def product_kernel(plan_ref, q0, q1, q2, q3, got_ref, b_ref, _, out_ref, res, acc, sems):
    count = plan_ref[PLAN_COUNT, 0]

    def product(entry):
        shift, at, i = (entry >> 2) & 3, entry & 3, (entry >> 20) & (RB - 1)
        left = jnp.where(
            shift < 2,
            jnp.where(shift == 0, q0[at, i], q1[at, i]),
            jnp.where(shift == 2, q2[at, i], q3[at, i]))
        source, place = (entry >> 4) & 15, (entry >> 8) & (KB - 1)
        near = source == LOCAL
        right = jnp.where(
            near, b_ref[jnp.where(near, place, 0)],
            got_ref[jnp.where(near, 0, source), jnp.where(near, 0, place)])
        return jnp.dot(left, right, preferred_element_type=jnp.float32)

    def step(number, written):
        sums = []
        for u in range(UNROLL):
            n = number * UNROLL + u
            entry = plan_ref[0, jnp.minimum(n, LANES - 1)]
            sums.append((n, entry, product(entry)))
        for n, entry, total in sums:
            hold = jnp.where(n < count, (entry >> 23) & (LANES - 1), LANES)
            total = total + jnp.where(hold < n, acc[hold], 0.0)
            acc[hold] = total
            res[hold] = total.astype(jnp.bfloat16)
            whole = (n < count) & ((entry >> 30) == 1)

            @pl.when(whole)
            def _():
                pltpu.make_async_copy(
                    res.at[hold], out_ref.at[(entry >> 20) & (RB - 1), (entry >> 14) & (JB - 1)],
                    sems.at[written]).start()

            written = written + whole.astype(jnp.int32)
        return written

    written = lax.fori_loop(0, (count + UNROLL - 1) // UNROLL, step, jnp.int32(0))

    @pl.loop(0, written)
    def _(n):
        pltpu.make_async_copy(res.at[0], out_ref.at[0, 0], sems.at[n]).wait()


def products(plan, left, got, b, blank):
    vmem = pl.BlockSpec(memory_space=pltpu.VMEM)
    place = pl.BlockSpec(memory_space=pl.ANY)
    return pl.pallas_call(
        product_kernel,
        out_shape=jax.ShapeDtypeStruct((RB, JB, BS, BS), jnp.bfloat16),
        in_specs=[pl.BlockSpec(memory_space=pltpu.SMEM)] + [vmem] * 6 + [place],
        out_specs=place,
        input_output_aliases={7: 0},
        scratch_shapes=[
            pltpu.VMEM((LANES + 1, BS, BS), jnp.bfloat16),
            pltpu.VMEM((LANES + 1, BS, BS), jnp.float32),
            pltpu.SemaphoreType.DMA((LANES,)),
        ],
        compiler_params=pltpu.CompilerParams(vmem_limit_bytes=44 << 20),
        name="block_products",
    )(plan, *left, got, b, blank)


def per_device(a_values, a_blocks, a_live, b_values, b_columns, filter_mask):
    me_r, me_c = lax.axis_index(R_AXES), lax.axis_index(C_AXES)
    a = a_values.reshape(RB, BS, BS)
    b = b_values.reshape(KB, BS, BS)

    def flipped(bits):
        return lax.ppermute(a, C_AXES, [(c, c ^ bits) for c in range(COLS)])

    record = make_record(
        (me_c * JB).astype(jnp.int32).reshape(1), a_blocks.reshape(1, RB), a_live.reshape(1, RB),
        b_columns.reshape(1, KB))
    record, a = lax.optimization_barrier((record, a))
    meta = lax.all_to_all(record, R_AXES + C_AXES, 0, 0, tiled=True)
    blank = zero_blocks()
    send, plan, which, quad = make_lists(
        me_r.astype(jnp.int32).reshape(1), me_c.astype(jnp.int32).reshape(1),
        meta.reshape(ROWS * COLS, LANES), filter_mask, [a, flipped(8), flipped(1), flipped(9)])

    def exchange(cap, first, send, b):
        return lax.all_to_all(pack(cap, first, send, b), R_AXES, 0, 0)

    def finish(plan, quad, b, blank, got):
        left = [quad] + [
            lax.ppermute(quad, "x", [(x, (x + shift) % 4) for x in range(4)])
            for shift in (1, 2, 3)]
        return products(plan, left, got, b, blank)

    def one_round(cap, which, send, plan, quad, b, blank):
        got = lax.cond(
            which >= 0, functools.partial(exchange, cap, 0), functools.partial(pack, cap, 0), send, b)
        return finish(plan, quad, b, blank, got)

    def rounds(which, send, plan, quad, b, blank):
        cap = CAPS[-1]
        got = [exchange(cap, first, send, b) for first in range(0, KB, cap)]
        return finish(plan, quad, b, blank, jnp.concatenate(got, axis=1))

    branches = [functools.partial(one_round, cap) for cap in CAPS] + [rounds]
    return lax.switch(which[0], branches, which[0], send, plan, quad, b, blank)


def solution(mesh):
    fine = Mesh(mesh.devices.reshape(4, 2, 2, 4, 2), R_AXES + C_AXES)
    pair = P(R_AXES, C_AXES)
    blocks = P(R_AXES, C_AXES, None, None)
    return jax.shard_map(
        per_device, mesh=fine, in_specs=(blocks, pair, pair, blocks, pair, pair),
        out_specs=blocks, check_vma=False
    )
```

```python
import functools

import jax
import jax.numpy as jnp
from jax import lax
from jax.experimental import pallas as pl
from jax.experimental.pallas import tpu as pltpu
from jax.sharding import Mesh, PartitionSpec as P

BS = 128
ROWS = 8
COLS = 16
RB = 8
KB = 64
JB = 64
SLOTS = 16
LANES = 128
CAPS = (12, 13, 14, 15, 16, 17, 18, 19, 20)
R_AXES = ("y", "zl")
C_AXES = ("zh", "x", "core")
UNROLL = 8

LOCAL = 8
PLAN_COUNT = 1


def record_kernel(base_ref, blocks_ref, live_ref, cols_ref, out_ref):
    keys = jnp.where(live_ref[...] != 0, blocks_ref[...], -1)
    row = jnp.concatenate(
        [keys, jnp.zeros((1, LANES - KB - RB), jnp.int32), cols_ref[...] - base_ref[0]], axis=1)
    out_ref[...] = jnp.broadcast_to(row.reshape(1, 1, LANES), out_ref.shape)


def make_record(base, blocks, live, cols):
    vmem = pl.BlockSpec(memory_space=pltpu.VMEM)
    return pl.pallas_call(
        record_kernel,
        out_shape=jax.ShapeDtypeStruct((ROWS * COLS, 1, LANES), jnp.int32),
        in_specs=[pl.BlockSpec(memory_space=pltpu.SMEM), vmem, vmem, vmem],
        out_specs=vmem,
        name="make_record",
    )(base, blocks, live, cols)


def list_kernel(r_ref, c_ref, meta_ref, mask_ref, a_ref, z_ref, k_ref, zk_ref,
                send_ref, plan_ref, which_ref, quad_ref, table_ref, quad_sems):
    copies = [
        pltpu.make_async_copy(ref, quad_ref.at[n], quad_sems.at[n])
        for n, ref in enumerate((a_ref, z_ref, k_ref, zk_ref))
    ]
    for copy in copies:
        copy.start()
    me_r, me_c = r_ref[0], c_ref[0]
    lane = lax.broadcasted_iota(jnp.int32, (LANES, LANES), 1)
    sub8 = lax.broadcasted_iota(jnp.int32, (ROWS, LANES), 0)
    lane8 = lax.broadcasted_iota(jnp.int32, (ROWS, LANES), 1)
    above = lax.broadcasted_iota(jnp.int32, (LANES, LANES), 0)
    before = ((above < lane) & (above // KB == lane // KB)).astype(jnp.float32)
    keys = meta_ref[:, 0:RB]
    top = jnp.zeros((ROWS, LANES), jnp.int32)

    def needed(base):
        hit = jnp.zeros((LANES, LANES), jnp.int32)
        for i in range(RB):
            hit = jnp.where(keys[:, i:i + 1] == lane + base, 1, hit)
        need = jnp.max(hit.reshape(ROWS, COLS, LANES), axis=1)
        rank = jnp.dot(need.astype(jnp.float32), before, preferred_element_type=jnp.float32)
        return need, rank.astype(jnp.int32)

    for q in range(ROWS * KB // LANES):
        need, rank = needed(q * LANES)
        owner = (lane8 + q * LANES) // KB
        top = jnp.maximum(top, jnp.where(owner == sub8, 0, need + rank))
        mine = jnp.sum(jnp.where(sub8 == me_r, rank, 0), axis=0, keepdims=True)
        low = meta_ref[pl.ds(2 * q * COLS + me_c, 1), :]
        high = meta_ref[pl.ds((2 * q + 1) * COLS + me_c, 1), :]
        cols = jnp.where(lane8[0:1] < KB, pltpu.roll(low, KB, 1), high)
        table_ref[q:q + 1, :] = mine * JB + cols
    largest = jnp.max(top)
    which_ref[0] = sum((largest > cap).astype(jnp.int32) for cap in CAPS)

    need, rank = needed(me_r * KB)
    need = jnp.where((lane8 < KB) & (sub8 != me_r), need, 0)
    counts = jnp.sum(need, axis=1, keepdims=True)

    def place(step, lists):
        for u in range(8):
            s = step * 8 + u
            here = jnp.sum(jnp.where((need == 1) & (rank == s), lane8, 0), axis=1, keepdims=True)
            lists = jnp.where(lane8 == s, here, lists)
        return lists

    lists = lax.fori_loop(0, (largest + 7) // 8, place, jnp.zeros((ROWS, LANES), jnp.int32))
    send_ref[...] = jnp.where(lane8 == LANES - 1, counts, lists)

    own = meta_ref[pl.ds(pl.multiple_of(me_r * COLS, COLS), COLS), :]
    lane16 = lax.broadcasted_iota(jnp.int32, (SLOTS, LANES), 1)
    sub16 = lax.broadcasted_iota(jnp.int32, (SLOTS, LANES), 0)
    lane_j = lax.broadcasted_iota(jnp.int32, (SLOTS, JB), 1)
    found = jnp.zeros((SLOTS, LANES), jnp.int32)
    kept = jnp.zeros((SLOTS, LANES), jnp.int32)
    for i in range(RB):
        key = own[:, i:i + 1]
        seen = jnp.zeros((SLOTS, LANES), jnp.int32)
        for q in range(ROWS * KB // LANES):
            seen = jnp.where(key == lane16 + q * LANES, table_ref[q:q + 1, :], seen)
        entry = jnp.sum(seen, axis=1, keepdims=True)
        keep = jnp.sum(jnp.where(lane_j == entry % JB, mask_ref[i:i + 1, :], 0), axis=1, keepdims=True)
        found = jnp.where(lane16 == i, entry, found)
        kept = jnp.where(lane16 == i, keep, kept)
    col, rank = found % JB, found // JB
    active = ((kept != 0) & (own >= 0) & (lane16 < RB)).astype(jnp.int32)
    pos = jnp.zeros((SLOTS, LANES), jnp.int32)
    for a in range(SLOTS):
        pos = pos + jnp.where(sub16 > a, active[a:a + 1, :], 0)
    first = jnp.full((SLOTS, LANES), SLOTS, jnp.int32)
    last = jnp.zeros((SLOTS, LANES), jnp.int32)
    for a in range(SLOTS):
        same = (active[a:a + 1, :] == 1) & (col[a:a + 1, :] == col)
        first = jnp.minimum(first, jnp.where(same, pos[a:a + 1, :], SLOTS))
        last = jnp.maximum(last, jnp.where(same, pos[a:a + 1, :], 0))
    in_row = jnp.sum(active, axis=0, keepdims=True)
    start = jnp.zeros((1, LANES), jnp.int32)
    for i in range(RB):
        start = start + jnp.where(lane8[0:1] > i, in_row[:, i:i + 1], 0)
    block, source = own & (KB - 1), own >> 6
    near = source == me_r
    other = sub16 ^ me_c
    left = ((((me_c >> 1) - (sub16 >> 1)) & 3) << 2) | ((other & 1) << 1) | ((other >> 3) & 1)
    packed = (left | (jnp.where(near, LOCAL, source) << 4) | (jnp.where(near, block, rank) << 8)
              | (col << 14) | (lane16 << 20) | ((start + first) << 23)
              | (jnp.where(last == pos, 1, 0) << 30))
    at = jnp.where(active == 1, start + pos, -1)
    listed = jnp.zeros((SLOTS, LANES), jnp.int32)
    for i in range(RB):
        listed = jnp.where(at[:, i:i + 1] == lane16, packed[:, i:i + 1], listed)
    plan_ref[0:1, :] = jnp.sum(listed, axis=0, keepdims=True)
    plan_ref[1:8, :] = jnp.broadcast_to(jnp.sum(in_row, axis=1, keepdims=True), (7, LANES))
    for copy in copies:
        copy.wait()


def make_lists(me_r, me_c, meta, mask, parts):
    vmem = pl.BlockSpec(memory_space=pltpu.VMEM)
    smem = pl.BlockSpec(memory_space=pltpu.SMEM)
    return pl.pallas_call(
        list_kernel,
        out_shape=(
            jax.ShapeDtypeStruct((ROWS, LANES), jnp.int32),
            jax.ShapeDtypeStruct((8, LANES), jnp.int32),
            jax.ShapeDtypeStruct((1,), jnp.int32),
            jax.ShapeDtypeStruct((4, RB, BS, BS), jnp.bfloat16),
        ),
        in_specs=[smem, smem] + [vmem] * 6,
        out_specs=(vmem, vmem, smem, pl.BlockSpec(memory_space=pl.ANY)),
        scratch_shapes=[
            pltpu.VMEM((ROWS * KB // LANES, LANES), jnp.int32),
            pltpu.SemaphoreType.DMA((4,)),
        ],
        compiler_params=pltpu.CompilerParams(vmem_limit_bytes=8 << 20),
        name="make_lists",
    )(me_r, me_c, meta, mask, *parts)


def pack_kernel(cap, first, send_ref, b_ref, out_ref, sems):
    def each(dest, go):
        count = jnp.clip(send_ref[dest, LANES - 1] - first, 0, cap)

        @pl.loop(0, count)
        def _(s):
            block = send_ref[dest, first + s]
            go(pltpu.make_async_copy(b_ref.at[block], out_ref.at[dest, s], sems.at[dest, s]))

    for dest in range(ROWS):
        each(dest, lambda copy: copy.start())
    for dest in range(ROWS):
        each(dest, lambda copy: copy.wait())


def pack(cap, first, send, b):
    return pl.pallas_call(
        functools.partial(pack_kernel, cap, first),
        out_shape=jax.ShapeDtypeStruct((ROWS, cap, BS, BS), jnp.bfloat16),
        in_specs=[
            pl.BlockSpec(memory_space=pltpu.SMEM),
            pl.BlockSpec(memory_space=pl.ANY),
        ],
        out_specs=pl.BlockSpec(memory_space=pltpu.VMEM),
        scratch_shapes=[pltpu.SemaphoreType.DMA((ROWS, cap))],
        compiler_params=pltpu.CompilerParams(vmem_limit_bytes=8 << 20),
        name="pack_blocks",
    )(send, b)


def zero_kernel(out_ref, zeros, sems):
    zeros[...] = jnp.zeros(zeros.shape, zeros.dtype)
    copies = [
        pltpu.make_async_copy(zeros, out_ref.at[i], sems.at[i]) for i in range(RB)
    ]
    for copy in copies:
        copy.start()
    for copy in copies:
        copy.wait()


def zero_blocks():
    return pl.pallas_call(
        zero_kernel,
        out_shape=jax.ShapeDtypeStruct((RB, JB, BS, BS), jnp.bfloat16),
        out_specs=pl.BlockSpec(memory_space=pl.ANY),
        scratch_shapes=[
            pltpu.VMEM((JB, BS, BS), jnp.bfloat16),
            pltpu.SemaphoreType.DMA((RB,)),
        ],
        compiler_params=pltpu.CompilerParams(vmem_limit_bytes=8 << 20),
        cost_estimate=pl.CostEstimate(flops=0, bytes_accessed=16 << 20, transcendentals=0),
        name="zero_blocks",
    )()


def product_kernel(plan_ref, q0, q1, q2, q3, got_ref, b_ref, _, out_ref, res, acc, sems):
    count = plan_ref[PLAN_COUNT, 0]

    def product(entry):
        shift, at, i = (entry >> 2) & 3, entry & 3, (entry >> 20) & (RB - 1)
        left = jnp.where(
            shift < 2,
            jnp.where(shift == 0, q0[at, i], q1[at, i]),
            jnp.where(shift == 2, q2[at, i], q3[at, i]))
        source, place = (entry >> 4) & 15, (entry >> 8) & (KB - 1)
        near = source == LOCAL
        right = jnp.where(
            near, b_ref[jnp.where(near, place, 0)],
            got_ref[jnp.where(near, 0, source), jnp.where(near, 0, place)])
        return jnp.dot(left, right, preferred_element_type=jnp.float32)

    def step(number, written):
        sums = []
        for u in range(UNROLL):
            n = number * UNROLL + u
            entry = plan_ref[0, jnp.minimum(n, LANES - 1)]
            sums.append((n, entry, product(entry)))
        for n, entry, total in sums:
            hold = jnp.where(n < count, (entry >> 23) & (LANES - 1), LANES)
            total = total + jnp.where(hold < n, acc[hold], 0.0)
            acc[hold] = total
            res[hold] = total.astype(jnp.bfloat16)
            whole = (n < count) & ((entry >> 30) == 1)

            @pl.when(whole)
            def _():
                pltpu.make_async_copy(
                    res.at[hold], out_ref.at[(entry >> 20) & (RB - 1), (entry >> 14) & (JB - 1)],
                    sems.at[written]).start()

            written = written + whole.astype(jnp.int32)
        return written

    written = lax.fori_loop(0, (count + UNROLL - 1) // UNROLL, step, jnp.int32(0))

    @pl.loop(0, written)
    def _(n):
        pltpu.make_async_copy(res.at[0], out_ref.at[0, 0], sems.at[n]).wait()


def products(plan, left, got, b, blank):
    vmem = pl.BlockSpec(memory_space=pltpu.VMEM)
    place = pl.BlockSpec(memory_space=pl.ANY)
    return pl.pallas_call(
        product_kernel,
        out_shape=jax.ShapeDtypeStruct((RB, JB, BS, BS), jnp.bfloat16),
        in_specs=[pl.BlockSpec(memory_space=pltpu.SMEM)] + [vmem] * 6 + [place],
        out_specs=place,
        input_output_aliases={7: 0},
        scratch_shapes=[
            pltpu.VMEM((LANES + 1, BS, BS), jnp.bfloat16),
            pltpu.VMEM((LANES + 1, BS, BS), jnp.float32),
            pltpu.SemaphoreType.DMA((LANES,)),
        ],
        compiler_params=pltpu.CompilerParams(vmem_limit_bytes=44 << 20),
        name="block_products",
    )(plan, *left, got, b, blank)


def per_device(a_values, a_blocks, a_live, b_values, b_columns, filter_mask):
    me_r, me_c = lax.axis_index(R_AXES), lax.axis_index(C_AXES)
    a = a_values.reshape(RB, BS, BS)
    b = b_values.reshape(KB, BS, BS)

    def flipped(bits):
        return lax.ppermute(a, C_AXES, [(c, c ^ bits) for c in range(COLS)])

    record = make_record(
        (me_c * JB).astype(jnp.int32).reshape(1), a_blocks.reshape(1, RB), a_live.reshape(1, RB),
        b_columns.reshape(1, KB))
    record, a = lax.optimization_barrier((record, a))
    meta = lax.all_to_all(record, R_AXES + C_AXES, 0, 0, tiled=True)
    blank = zero_blocks()
    send, plan, which, quad = make_lists(
        me_r.astype(jnp.int32).reshape(1), me_c.astype(jnp.int32).reshape(1),
        meta.reshape(ROWS * COLS, LANES), filter_mask, [a, flipped(8), flipped(1), flipped(9)])

    def exchange(cap, first, send, b):
        return lax.all_to_all(pack(cap, first, send, b), R_AXES, 0, 0)

    def finish(plan, quad, b, blank, got):
        left = [quad] + [
            lax.ppermute(quad, "x", [(x, (x + shift) % 4) for x in range(4)])
            for shift in (1, 2, 3)]
        return products(plan, left, got, b, blank)

    def one_round(cap, which, send, plan, quad, b, blank):
        got = lax.cond(
            which >= 0, functools.partial(exchange, cap, 0), functools.partial(pack, cap, 0), send, b)
        return finish(plan, quad, b, blank, got)

    def rounds(which, send, plan, quad, b, blank):
        cap = CAPS[-1]
        got = [exchange(cap, first, send, b) for first in range(0, KB, cap)]
        return finish(plan, quad, b, blank, jnp.concatenate(got, axis=1))

    branches = [functools.partial(one_round, cap) for cap in CAPS] + [rounds]
    return lax.switch(which[0], branches, which[0], send, plan, quad, b, blank)


def solution(mesh):
    fine = Mesh(mesh.devices.reshape(4, 2, 2, 4, 2), R_AXES + C_AXES)
    pair = P(R_AXES, C_AXES)
    blocks = P(R_AXES, C_AXES, None, None)
    return jax.shard_map(
        per_device, mesh=fine, in_specs=(blocks, pair, pair, blocks, pair, pair),
        out_specs=blocks, check_vma=False
    )
```

```python
import functools

import jax
import jax.numpy as jnp
from jax import lax
from jax.experimental import pallas as pl
from jax.experimental.pallas import tpu as pltpu
from jax.sharding import Mesh, PartitionSpec as P

BS = 128
ROWS = 8
COLS = 16
RB = 8
KB = 64
JB = 64
SLOTS = 16
LANES = 128
CAPS = (13, 14, 15, 16, 17, 18, 20)
R_AXES = ("y", "zl")
C_AXES = ("zh", "x", "core")
UNROLL = 8

LOCAL = 8
PLAN_COUNT = 1


def record_kernel(base_ref, blocks_ref, live_ref, cols_ref, out_ref):
    keys = jnp.where(live_ref[...] != 0, blocks_ref[...], -1)
    row = jnp.concatenate(
        [keys, jnp.zeros((1, LANES - KB - RB), jnp.int32), cols_ref[...] - base_ref[0]], axis=1)
    out_ref[...] = jnp.broadcast_to(row.reshape(1, 1, LANES), out_ref.shape)


def make_record(base, blocks, live, cols):
    vmem = pl.BlockSpec(memory_space=pltpu.VMEM)
    return pl.pallas_call(
        record_kernel,
        out_shape=jax.ShapeDtypeStruct((ROWS * COLS, 1, LANES), jnp.int32),
        in_specs=[pl.BlockSpec(memory_space=pltpu.SMEM), vmem, vmem, vmem],
        out_specs=vmem,
        name="make_record",
    )(base, blocks, live, cols)


def list_kernel(r_ref, c_ref, meta_ref, mask_ref, a_ref, z_ref, k_ref, zk_ref,
                send_ref, plan_ref, which_ref, quad_ref, table_ref, quad_sems):
    copies = [
        pltpu.make_async_copy(ref, quad_ref.at[n], quad_sems.at[n])
        for n, ref in enumerate((a_ref, z_ref, k_ref, zk_ref))
    ]
    for copy in copies:
        copy.start()
    me_r, me_c = r_ref[0], c_ref[0]
    lane = lax.broadcasted_iota(jnp.int32, (LANES, LANES), 1)
    sub8 = lax.broadcasted_iota(jnp.int32, (ROWS, LANES), 0)
    lane8 = lax.broadcasted_iota(jnp.int32, (ROWS, LANES), 1)
    above = lax.broadcasted_iota(jnp.int32, (LANES, LANES), 0)
    before = ((above < lane) & (above // KB == lane // KB)).astype(jnp.float32)
    keys = meta_ref[:, 0:RB]
    top = jnp.zeros((ROWS, LANES), jnp.int32)

    def needed(base):
        hit = jnp.zeros((LANES, LANES), jnp.int32)
        for i in range(RB):
            hit = jnp.where(keys[:, i:i + 1] == lane + base, 1, hit)
        need = jnp.max(hit.reshape(ROWS, COLS, LANES), axis=1)
        rank = jnp.dot(need.astype(jnp.float32), before, preferred_element_type=jnp.float32)
        return need, rank.astype(jnp.int32)

    for q in range(ROWS * KB // LANES):
        need, rank = needed(q * LANES)
        owner = (lane8 + q * LANES) // KB
        top = jnp.maximum(top, jnp.where(owner == sub8, 0, need + rank))
        mine = jnp.sum(jnp.where(sub8 == me_r, rank, 0), axis=0, keepdims=True)
        low = meta_ref[pl.ds(2 * q * COLS + me_c, 1), :]
        high = meta_ref[pl.ds((2 * q + 1) * COLS + me_c, 1), :]
        cols = jnp.where(lane8[0:1] < KB, pltpu.roll(low, KB, 1), high)
        table_ref[q:q + 1, :] = mine * JB + cols
    largest = jnp.max(top)
    which_ref[0] = sum((largest > cap).astype(jnp.int32) for cap in CAPS)

    need, rank = needed(me_r * KB)
    need = jnp.where((lane8 < KB) & (sub8 != me_r), need, 0)
    counts = jnp.sum(need, axis=1, keepdims=True)

    def place(step, lists):
        for u in range(8):
            s = step * 8 + u
            here = jnp.sum(jnp.where((need == 1) & (rank == s), lane8, 0), axis=1, keepdims=True)
            lists = jnp.where(lane8 == s, here, lists)
        return lists

    lists = lax.fori_loop(0, (largest + 7) // 8, place, jnp.zeros((ROWS, LANES), jnp.int32))
    send_ref[...] = jnp.where(lane8 == LANES - 1, counts, lists)

    own = meta_ref[pl.ds(pl.multiple_of(me_r * COLS, COLS), COLS), :]
    lane16 = lax.broadcasted_iota(jnp.int32, (SLOTS, LANES), 1)
    sub16 = lax.broadcasted_iota(jnp.int32, (SLOTS, LANES), 0)
    lane_j = lax.broadcasted_iota(jnp.int32, (SLOTS, JB), 1)
    found = jnp.zeros((SLOTS, LANES), jnp.int32)
    kept = jnp.zeros((SLOTS, LANES), jnp.int32)
    for i in range(RB):
        key = own[:, i:i + 1]
        seen = jnp.zeros((SLOTS, LANES), jnp.int32)
        for q in range(ROWS * KB // LANES):
            seen = jnp.where(key == lane16 + q * LANES, table_ref[q:q + 1, :], seen)
        entry = jnp.sum(seen, axis=1, keepdims=True)
        keep = jnp.sum(jnp.where(lane_j == entry % JB, mask_ref[i:i + 1, :], 0), axis=1, keepdims=True)
        found = jnp.where(lane16 == i, entry, found)
        kept = jnp.where(lane16 == i, keep, kept)
    col, rank = found % JB, found // JB
    active = ((kept != 0) & (own >= 0) & (lane16 < RB)).astype(jnp.int32)
    pos = jnp.zeros((SLOTS, LANES), jnp.int32)
    for a in range(SLOTS):
        pos = pos + jnp.where(sub16 > a, active[a:a + 1, :], 0)
    first = jnp.full((SLOTS, LANES), SLOTS, jnp.int32)
    last = jnp.zeros((SLOTS, LANES), jnp.int32)
    for a in range(SLOTS):
        same = (active[a:a + 1, :] == 1) & (col[a:a + 1, :] == col)
        first = jnp.minimum(first, jnp.where(same, pos[a:a + 1, :], SLOTS))
        last = jnp.maximum(last, jnp.where(same, pos[a:a + 1, :], 0))
    in_row = jnp.sum(active, axis=0, keepdims=True)
    start = jnp.zeros((1, LANES), jnp.int32)
    for i in range(RB):
        start = start + jnp.where(lane8[0:1] > i, in_row[:, i:i + 1], 0)
    block, source = own & (KB - 1), own >> 6
    near = source == me_r
    other = sub16 ^ me_c
    left = ((((me_c >> 1) - (sub16 >> 1)) & 3) << 2) | ((other & 1) << 1) | ((other >> 3) & 1)
    packed = (left | (jnp.where(near, LOCAL, source) << 4) | (jnp.where(near, block, rank) << 8)
              | (col << 14) | (lane16 << 20) | ((start + first) << 23)
              | (jnp.where(last == pos, 1, 0) << 30))
    at = jnp.where(active == 1, start + pos, -1)
    listed = jnp.zeros((SLOTS, LANES), jnp.int32)
    for i in range(RB):
        listed = jnp.where(at[:, i:i + 1] == lane16, packed[:, i:i + 1], listed)
    plan_ref[0:1, :] = jnp.sum(listed, axis=0, keepdims=True)
    plan_ref[1:8, :] = jnp.broadcast_to(jnp.sum(in_row, axis=1, keepdims=True), (7, LANES))
    for copy in copies:
        copy.wait()


def make_lists(me_r, me_c, meta, mask, parts):
    vmem = pl.BlockSpec(memory_space=pltpu.VMEM)
    smem = pl.BlockSpec(memory_space=pltpu.SMEM)
    return pl.pallas_call(
        list_kernel,
        out_shape=(
            jax.ShapeDtypeStruct((ROWS, LANES), jnp.int32),
            jax.ShapeDtypeStruct((8, LANES), jnp.int32),
            jax.ShapeDtypeStruct((1,), jnp.int32),
            jax.ShapeDtypeStruct((4, RB, BS, BS), jnp.bfloat16),
        ),
        in_specs=[smem, smem] + [vmem] * 6,
        out_specs=(vmem, vmem, smem, pl.BlockSpec(memory_space=pl.ANY)),
        scratch_shapes=[
            pltpu.VMEM((ROWS * KB // LANES, LANES), jnp.int32),
            pltpu.SemaphoreType.DMA((4,)),
        ],
        compiler_params=pltpu.CompilerParams(vmem_limit_bytes=8 << 20),
        name="make_lists",
    )(me_r, me_c, meta, mask, *parts)


def pack_kernel(cap, first, send_ref, b_ref, out_ref, sems):
    def each(dest, go):
        count = jnp.clip(send_ref[dest, LANES - 1] - first, 0, cap)

        @pl.loop(0, count)
        def _(s):
            block = send_ref[dest, first + s]
            go(pltpu.make_async_copy(b_ref.at[block], out_ref.at[dest, s], sems.at[dest, s]))

    for dest in range(ROWS):
        each(dest, lambda copy: copy.start())
    for dest in range(ROWS):
        each(dest, lambda copy: copy.wait())


def pack(cap, first, send, b):
    return pl.pallas_call(
        functools.partial(pack_kernel, cap, first),
        out_shape=jax.ShapeDtypeStruct((ROWS, cap, BS, BS), jnp.bfloat16),
        in_specs=[
            pl.BlockSpec(memory_space=pltpu.SMEM),
            pl.BlockSpec(memory_space=pl.ANY),
        ],
        out_specs=pl.BlockSpec(memory_space=pltpu.VMEM),
        scratch_shapes=[pltpu.SemaphoreType.DMA((ROWS, cap))],
        compiler_params=pltpu.CompilerParams(vmem_limit_bytes=8 << 20),
        name="pack_blocks",
    )(send, b)


def zero_kernel(out_ref, zeros, sems):
    zeros[...] = jnp.zeros(zeros.shape, zeros.dtype)
    copies = [
        pltpu.make_async_copy(zeros, out_ref.at[i], sems.at[i]) for i in range(RB)
    ]
    for copy in copies:
        copy.start()
    for copy in copies:
        copy.wait()


def zero_blocks():
    return pl.pallas_call(
        zero_kernel,
        out_shape=jax.ShapeDtypeStruct((RB, JB, BS, BS), jnp.bfloat16),
        out_specs=pl.BlockSpec(memory_space=pl.ANY),
        scratch_shapes=[
            pltpu.VMEM((JB, BS, BS), jnp.bfloat16),
            pltpu.SemaphoreType.DMA((RB,)),
        ],
        compiler_params=pltpu.CompilerParams(vmem_limit_bytes=8 << 20),
        cost_estimate=pl.CostEstimate(flops=0, bytes_accessed=16 << 20, transcendentals=0),
        name="zero_blocks",
    )()


def product_kernel(plan_ref, q0, q1, q2, q3, got_ref, b_ref, _, out_ref, res, acc, sems):
    count = plan_ref[PLAN_COUNT, 0]

    def product(entry):
        shift, at, i = (entry >> 2) & 3, entry & 3, (entry >> 20) & (RB - 1)
        left = jnp.where(
            shift < 2,
            jnp.where(shift == 0, q0[at, i], q1[at, i]),
            jnp.where(shift == 2, q2[at, i], q3[at, i]))
        source, place = (entry >> 4) & 15, (entry >> 8) & (KB - 1)
        near = source == LOCAL
        right = jnp.where(
            near, b_ref[jnp.where(near, place, 0)],
            got_ref[jnp.where(near, 0, source), jnp.where(near, 0, place)])
        return jnp.dot(left, right, preferred_element_type=jnp.float32)

    def step(number, written):
        sums = []
        for u in range(UNROLL):
            n = number * UNROLL + u
            entry = plan_ref[0, jnp.minimum(n, LANES - 1)]
            sums.append((n, entry, product(entry)))
        for n, entry, total in sums:
            hold = jnp.where(n < count, (entry >> 23) & (LANES - 1), LANES)
            total = total + jnp.where(hold < n, acc[hold], 0.0)
            acc[hold] = total
            res[hold] = total.astype(jnp.bfloat16)
            whole = (n < count) & ((entry >> 30) == 1)

            @pl.when(whole)
            def _():
                pltpu.make_async_copy(
                    res.at[hold], out_ref.at[(entry >> 20) & (RB - 1), (entry >> 14) & (JB - 1)],
                    sems.at[written]).start()

            written = written + whole.astype(jnp.int32)
        return written

    written = lax.fori_loop(0, (count + UNROLL - 1) // UNROLL, step, jnp.int32(0))

    @pl.loop(0, written)
    def _(n):
        pltpu.make_async_copy(res.at[0], out_ref.at[0, 0], sems.at[n]).wait()


def products(plan, left, got, b, blank):
    vmem = pl.BlockSpec(memory_space=pltpu.VMEM)
    place = pl.BlockSpec(memory_space=pl.ANY)
    return pl.pallas_call(
        product_kernel,
        out_shape=jax.ShapeDtypeStruct((RB, JB, BS, BS), jnp.bfloat16),
        in_specs=[pl.BlockSpec(memory_space=pltpu.SMEM)] + [vmem] * 6 + [place],
        out_specs=place,
        input_output_aliases={7: 0},
        scratch_shapes=[
            pltpu.VMEM((LANES + 1, BS, BS), jnp.bfloat16),
            pltpu.VMEM((LANES + 1, BS, BS), jnp.float32),
            pltpu.SemaphoreType.DMA((LANES,)),
        ],
        compiler_params=pltpu.CompilerParams(vmem_limit_bytes=44 << 20),
        name="block_products",
    )(plan, *left, got, b, blank)


def per_device(a_values, a_blocks, a_live, b_values, b_columns, filter_mask):
    me_r, me_c = lax.axis_index(R_AXES), lax.axis_index(C_AXES)
    a = a_values.reshape(RB, BS, BS)
    b = b_values.reshape(KB, BS, BS)

    def flipped(bits):
        return lax.ppermute(a, C_AXES, [(c, c ^ bits) for c in range(COLS)])

    record = make_record(
        (me_c * JB).astype(jnp.int32).reshape(1), a_blocks.reshape(1, RB), a_live.reshape(1, RB),
        b_columns.reshape(1, KB))
    record, a = lax.optimization_barrier((record, a))
    meta = lax.all_to_all(record, R_AXES + C_AXES, 0, 0, tiled=True)
    blank = zero_blocks()
    send, plan, which, quad = make_lists(
        me_r.astype(jnp.int32).reshape(1), me_c.astype(jnp.int32).reshape(1),
        meta.reshape(ROWS * COLS, LANES), filter_mask, [a, flipped(8), flipped(1), flipped(9)])

    def exchange(cap, first, send, b):
        return lax.all_to_all(pack(cap, first, send, b), R_AXES, 0, 0)

    def finish(plan, quad, b, blank, got):
        left = [quad] + [
            lax.ppermute(quad, "x", [(x, (x + shift) % 4) for x in range(4)])
            for shift in (1, 2, 3)]
        return products(plan, left, got, b, blank)

    def one_round(cap, send, plan, quad, b, blank):
        got = lax.cond(
            lax.axis_index("y") >= 0, functools.partial(exchange, cap, 0), functools.partial(pack, cap, 0), send, b)
        return finish(plan, quad, b, blank, got)

    def rounds(send, plan, quad, b, blank):
        cap = CAPS[-1]
        got = [exchange(cap, first, send, b) for first in range(0, KB, cap)]
        return finish(plan, quad, b, blank, jnp.concatenate(got, axis=1))

    branches = [functools.partial(one_round, cap) for cap in CAPS] + [rounds]
    return lax.switch(which[0], branches, send, plan, quad, b, blank)


def solution(mesh):
    fine = Mesh(mesh.devices.reshape(4, 2, 2, 4, 2), R_AXES + C_AXES)
    pair = P(R_AXES, C_AXES)
    blocks = P(R_AXES, C_AXES, None, None)
    return jax.shard_map(
        per_device, mesh=fine, in_specs=(blocks, pair, pair, blocks, pair, pair),
        out_specs=blocks, check_vma=False
    )
```
